512 devices in a mesh: tm: 8 (over x, core), dom: 64 (over y, z).
Axes of the slice: x: 4, y: 4, z: 16, core: 2. Of those that a mesh axis runs over, the one named last changes fastest.
Arguments:
- memory_start: bfloat16 [131072, 256], P('dom'), may hold values from -40 to 40
- src_row: int32 [8, 16384], P('tm', 'dom'), may hold values from 0 to 2047
- dst_pos: int32 [8, 16384], P('tm', 'dom'), may hold values from 0 to 8191, as said below
- neg_pos: int32 [8, 16384], P('tm', 'dom'), may hold values from 0 to 8191, as said below
- nbr_pos: int32 [8, 16384, 32], P('tm', 'dom'), may hold values from 0 to 8191, as said below
- event_time: int32 [8, 16384], P('tm', 'dom'), may hold values from 4096 to 8191
- nbr_time: int32 [8, 16384, 32], P('tm', 'dom'), may hold values from 0 to 4095
- edge_feat: bfloat16 [8, 16384, 172], P('tm', 'dom'), may hold values from -6 to 6
- tile_req: int32 [8, 64, 64], P('tm', 'dom'), may hold values from 0 to 15
- tile_count: int32 [8, 64, 64], P('tm', 'dom'), may hold values from 0 to 1, as said below
- time_freq: float32 [128], replicated, may hold values from 0.0001 to 0.3
- time_phase: float32 [128], replicated, may hold values from -3.140625 to 3.140625
- msg_memory: bfloat16 [512, 768], replicated, may hold values from -0.21875 to 0.21875
- msg_time: bfloat16 [128, 768], replicated, may hold values from -0.21875 to 0.21875
- msg_edge: bfloat16 [172, 768], replicated, may hold values from -0.21875 to 0.21875
- bias_input: float32 [768], replicated, may hold values from -3 to 3
- hid_weight: bfloat16 [256, 768], replicated, may hold values from -0.375 to 0.375
- bias_hidden: float32 [768], replicated, may hold values from -3 to 3
- query_weight: bfloat16 [256, 256], replicated, may hold values from -0.375 to 0.375
- keyval_weight: bfloat16 [384, 512], replicated, may hold values from -0.3125 to 0.3125
- out_weight: bfloat16 [512, 256], replicated, may hold values from -0.25 to 0.25
- bias_out: float32 [256], replicated, may hold values from -3 to 3
- pred_weight: bfloat16 [512, 256], replicated, may hold values from -0.25 to 0.25
- bias_pred: float32 [256], replicated, may hold values from -3 to 3
- logit_weight: bfloat16 [256], replicated, may hold values from -0.375 to 0.375
Outputs:
- logits: float32 [2, 8, 16384], P(None, 'tm', 'dom')
- memory_after: bfloat16 [8, 131072, 256], P('tm', 'dom')
The draws below stay inside these ranges and needn't reach their ends.
Inputs may be any that keep to these rules, and one draw needn't show every extreme that they name: `tile_count`: 0 or 1; in each batch one owner has count 1 from every device, and one device has count 1 for every owner. `dst_pos`: below 128 times the number of owners with tile count 1 for the event's device and batch; that bound minus one is taken by some event of every device in every batch. `neg_pos`: below 128 times the number of owners with tile count 1 for the event's device and batch; that bound minus one is taken by some event of every device in every batch. `nbr_pos`: below 128 times the number of owners with tile count 1 for the event's device and batch; that bound minus one is taken by some neighbour on every device in every batch.
All inputs are finite; a program needn't handle non-finite values.
Results may differ from the reference program's by a relative error of at most 0.0075.
Values may be sent and summed in bfloat16 or wider, within the bound.
No kernel may reach another device: no remote copies, remote signals or barrier semaphores. Data moves between devices by JAX's collectives and lax.ppermute only.
A program may use at most 192 MiB of HBM per device.

```python
import math
import jax
import jax.numpy as jnp
from jax import lax

D_MEM = 256
EDGE = 172
TE = 128
HEADS = 2
NBR = 32
TILE = 128
TIME_SPAN = 4096
TILES_DEV = 16
EV_DEV = 256
BATCHES = 8
OWNERS = 64
BATCH = 16384
NODES_DEV = 2048
NODES = 131072


def tile_counts(key):
    own_key = jax.random.fold_in(key, 7001)
    hot_key, base_key, full_key = jax.random.split(own_key, 3)
    hottest = jax.random.randint(hot_key, (BATCHES, 1, 1), 0, OWNERS)
    fullest = jax.random.randint(full_key, (BATCHES, 1, 1), 0, OWNERS)
    chosen = (jax.random.randint(base_key, (BATCHES, OWNERS, OWNERS), 0, 5) < 3).astype(jnp.int32)
    owner_ids = jnp.arange(OWNERS, dtype=jnp.int32)[None, None, :]
    device_ids = jnp.arange(OWNERS, dtype=jnp.int32)[None, :, None]
    marked = (owner_ids == hottest) | (device_ids == fullest)
    return jnp.where(marked, 1, chosen).astype(jnp.int32)


def event_limits(key):
    used_tiles = jnp.sum(tile_counts(key), axis=2)
    return jnp.repeat(used_tiles, EV_DEV, axis=1) * TILE


def top_events(key):
    picked = jax.random.randint(key, (BATCHES, OWNERS, 1), 0, EV_DEV)
    event_ids = jnp.arange(EV_DEV, dtype=jnp.int32)[None, None, :]
    return (event_ids == picked).reshape(BATCHES, BATCH)


def draw_tile_count(key, part):
    return tile_counts(key)


def draw_dst_pos(key, part):
    limits = event_limits(key)
    key = jax.random.fold_in(key, 11)
    value_key, top_key = jax.random.split(key)
    values = jax.random.randint(value_key, (BATCHES, BATCH), 0, limits)
    return jnp.where(top_events(top_key), limits - 1, values).astype(jnp.int32)


def draw_neg_pos(key, part):
    limits = event_limits(key)
    key = jax.random.fold_in(key, 13)
    value_key, top_key = jax.random.split(key)
    values = jax.random.randint(value_key, (BATCHES, BATCH), 0, limits)
    return jnp.where(top_events(top_key), limits - 1, values).astype(jnp.int32)


def draw_nbr_pos(key, part):
    limits = event_limits(key)
    key = jax.random.fold_in(key, 17)
    value_key, top_key, slot_key = jax.random.split(key, 3)
    values = jax.random.randint(value_key, (BATCHES, BATCH, NBR), 0, limits[:, :, None])
    slot = jax.random.randint(slot_key, (BATCHES, BATCH, 1), 0, NBR)
    slot_ids = jnp.arange(NBR, dtype=jnp.int32)[None, None, :]
    marked = top_events(top_key)[:, :, None] & (slot_ids == slot)
    return jnp.where(marked, limits[:, :, None] - 1, values).astype(jnp.int32)


def draw_memory_start(key, part):
    key = jax.random.fold_in(key, 31)
    first_key = jax.random.fold_in(key, 0)
    values = jnp.clip(jax.random.normal(first_key, (NODES, D_MEM), jnp.float32), -6.0, 6.0)
    return values.astype(jnp.bfloat16)


def set_ends(result, rng, low, top_value):
    longest = result.shape.index(max(result.shape))
    spots = []
    for shift in (0, 1):
        where = [jax.random.randint(jax.random.fold_in(rng, axis), (), 0, length) for axis, length in enumerate(result.shape)]
        where[longest] = (where[longest] + shift) % result.shape[longest]
        spots.append(tuple(where))
    return result.at[spots[0]].set(low).at[spots[1]].set(top_value)


def shard_levels(key, dims, pieces, low, largest):
    level = 1.0
    for dim, parts in pieces:
        heights = jax.random.uniform(jax.random.fold_in(jax.random.fold_in(key, 6), dim), (parts,), jnp.float32, low / len(pieces), largest / len(pieces))
        level = level * jnp.repeat(jnp.exp(heights), dims[dim] // parts).reshape((-1,) + (1,) * (len(dims) - 1 - dim))
    return level


def noise(key, extent, deviation, limit, shards=(), kind=jnp.bfloat16):
    result = deviation * jax.random.normal(key, extent, jnp.float32)
    if shards:
        result = result * shard_levels(key, extent, shards, -0.22, 0.18)
    return jnp.clip(result, -limit, limit).astype(kind)


def setup_inputs(seed: int = 0) -> dict:
    keys = jax.random.split(jax.random.key(seed), 26)
    memory_start = draw_memory_start(jax.random.fold_in(keys[25], 71), 0)
    src_row = set_ends(jax.random.randint(keys[1], (BATCHES, BATCH), 0, NODES_DEV), jax.random.fold_in(keys[1], 1), 0, NODES_DEV - 1).astype(jnp.int32)
    dst_pos = draw_dst_pos(jax.random.fold_in(keys[25], 71), 0)
    neg_pos = draw_neg_pos(jax.random.fold_in(keys[25], 71), 0)
    nbr_pos = draw_nbr_pos(jax.random.fold_in(keys[25], 71), 0)
    event_time = set_ends(jax.random.randint(keys[5], (BATCHES, BATCH), TIME_SPAN, 2 * TIME_SPAN), jax.random.fold_in(keys[5], 1), TIME_SPAN, (2 * TIME_SPAN) - 1).astype(jnp.int32)
    nbr_time = set_ends(jax.random.randint(keys[6], (BATCHES, BATCH, NBR), 0, TIME_SPAN), jax.random.fold_in(keys[6], 1), 0, TIME_SPAN - 1).astype(jnp.int32)
    edge_feat = noise(keys[7], (BATCHES, BATCH, EDGE), 1.0, 6.0, ((0, 8), (1, 64)))
    tile_req = set_ends(jax.random.randint(keys[8], (BATCHES, OWNERS, OWNERS), 0, TILES_DEV), jax.random.fold_in(keys[8], 1), 0, TILES_DEV - 1).astype(jnp.int32)
    tile_count = draw_tile_count(jax.random.fold_in(keys[25], 71), 0)
    time_freq = jnp.clip(jnp.exp(jax.random.uniform(keys[10], (TE,), jnp.float32, math.log(0.0001), math.log(0.3))), 0.0001, 0.3)
    time_phase = jnp.clip(jax.random.uniform(keys[11], (TE,), jnp.float32, -3.140625, 3.140625), -3.140625, 3.140625)
    msg_memory = noise(keys[12], (2 * D_MEM, 3 * D_MEM), (2 * D_MEM + TE + EDGE) ** -0.5, 0.21875)
    msg_time = noise(keys[13], (TE, 3 * D_MEM), (2 * D_MEM + TE + EDGE) ** -0.5, 0.21875)
    msg_edge = noise(keys[14], (EDGE, 3 * D_MEM), (2 * D_MEM + TE + EDGE) ** -0.5, 0.21875)
    bias_input = noise(keys[15], (3 * D_MEM,), 0.5, 3.0, (), jnp.float32)
    hid_weight = noise(keys[16], (D_MEM, 3 * D_MEM), D_MEM ** -0.5, 0.375)
    bias_hidden = noise(keys[17], (3 * D_MEM,), 0.5, 3.0, (), jnp.float32)
    query_weight = noise(keys[18], (D_MEM, D_MEM), D_MEM ** -0.5, 0.375)
    keyval_weight = noise(keys[19], (D_MEM + TE, 2 * D_MEM), (D_MEM + TE) ** -0.5, 0.3125)
    out_weight = noise(keys[20], (2 * D_MEM, D_MEM), (2 * D_MEM) ** -0.5, 0.25)
    bias_out = noise(keys[21], (D_MEM,), 0.5, 3.0, (), jnp.float32)
    pred_weight = noise(keys[22], (2 * D_MEM, D_MEM), (2 * D_MEM) ** -0.5, 0.25)
    bias_pred = noise(keys[23], (D_MEM,), 0.5, 3.0, (), jnp.float32)
    logit_weight = noise(keys[24], (D_MEM,), D_MEM ** -0.5, 0.375)
    return dict(memory_start=memory_start, src_row=src_row, dst_pos=dst_pos, neg_pos=neg_pos, nbr_pos=nbr_pos, event_time=event_time, nbr_time=nbr_time, edge_feat=edge_feat, tile_req=tile_req, tile_count=tile_count, time_freq=time_freq, time_phase=time_phase, msg_memory=msg_memory, msg_time=msg_time, msg_edge=msg_edge, bias_input=bias_input, hid_weight=hid_weight, bias_hidden=bias_hidden, query_weight=query_weight, keyval_weight=keyval_weight, out_weight=out_weight, bias_out=bias_out, pred_weight=pred_weight, bias_pred=bias_pred, logit_weight=logit_weight)


def time_code(delta, time_freq, time_phase):
    angle = delta.astype(jnp.float32)[..., None] * time_freq + time_phase
    return jnp.cos(angle).astype(jnp.bfloat16)

def global_nodes(position, wanted, counts):
    running = jnp.cumsum(counts)
    tile_index = position // TILE
    owner_id = lax.optimization_barrier(jnp.sum((running <= tile_index[..., None]).astype(jnp.int32), axis=-1))
    return (owner_id * NODES_DEV + wanted[owner_id] * TILE + position % TILE).astype(jnp.int32)

def gru_update(gate_in, gate_hid, state):
    state_width = state.shape[1]
    reset_gate = jax.nn.sigmoid(gate_in[:, :state_width] + gate_hid[:, :state_width])
    keep_gate = jax.nn.sigmoid(gate_in[:, state_width:2 * state_width] + gate_hid[:, state_width:2 * state_width])
    candidate = jnp.tanh(gate_in[:, 2 * state_width:] + reset_gate * gate_hid[:, 2 * state_width:])
    return (1.0 - keep_gate) * candidate + keep_gate * state.astype(jnp.float32)

def reference(memory_start, src_row, dst_pos, neg_pos, nbr_pos, event_time, nbr_time, edge_feat, tile_req, tile_count, time_freq, time_phase, msg_memory, msg_time, msg_edge, bias_input, hid_weight, bias_hidden, query_weight, keyval_weight, out_weight, bias_out, pred_weight, bias_pred, logit_weight):
    span_values = jnp.arange(2 * TIME_SPAN, dtype=jnp.int32)
    code_table = time_code(span_values, time_freq, time_phase)
    time_keys = jnp.dot(code_table, keyval_weight[D_MEM:], preferred_element_type=jnp.float32)
    memory_keys = jnp.dot(memory_start, keyval_weight[:D_MEM], preferred_element_type=jnp.float32)
    hidden_gates = jnp.dot(memory_start, hid_weight, preferred_element_type=jnp.float32) + bias_hidden
    head_width = D_MEM // HEADS
    current = memory_start
    all_logits = []
    all_memory = []
    for batch_index in range(BATCHES):

        def device_step(owner_index):
            first_event = owner_index * EV_DEV
            first_node = owner_index * NODES_DEV
            sources = lax.dynamic_slice_in_dim(src_row[batch_index], first_event, EV_DEV, 0)
            dst_here = lax.dynamic_slice_in_dim(dst_pos[batch_index], first_event, EV_DEV, 0)
            neg_here = lax.dynamic_slice_in_dim(neg_pos[batch_index], first_event, EV_DEV, 0)
            nbr_here = lax.dynamic_slice_in_dim(nbr_pos[batch_index], first_event, EV_DEV, 0)
            event_times = lax.dynamic_slice_in_dim(event_time[batch_index], first_event, EV_DEV, 0)
            past_times = lax.dynamic_slice_in_dim(nbr_time[batch_index], first_event, EV_DEV, 0)
            edges_here = lax.dynamic_slice_in_dim(edge_feat[batch_index], first_event, EV_DEV, 0)
            wanted = tile_req[batch_index][owner_index]
            counts = tile_count[batch_index][owner_index]
            start_block = lax.dynamic_slice_in_dim(memory_start, first_node, NODES_DEV, 0)
            current_block = lax.dynamic_slice_in_dim(current, first_node, NODES_DEV, 0)
            gate_block = lax.dynamic_slice_in_dim(hidden_gates, first_node, NODES_DEV, 0)
            dst_nodes = global_nodes(dst_here, wanted, counts)
            neg_nodes = global_nodes(neg_here, wanted, counts)
            nbr_nodes = global_nodes(nbr_here, wanted, counts)
            source_mem = start_block[sources]
            target_mem = memory_start[dst_nodes]
            message_code = code_table[event_times - past_times[:, 0]]
            pre_gate = jnp.dot(source_mem, msg_memory[:D_MEM], preferred_element_type=jnp.float32)
            pre_gate = pre_gate + jnp.dot(target_mem, msg_memory[D_MEM:], preferred_element_type=jnp.float32)
            pre_gate = pre_gate + jnp.dot(message_code, msg_time, preferred_element_type=jnp.float32)
            pre_gate = pre_gate + jnp.dot(edges_here, msg_edge, preferred_element_type=jnp.float32)
            pre_gate = pre_gate + bias_input
            summed = jax.ops.segment_sum(pre_gate, sources, num_segments=NODES_DEV)
            tallies = jax.ops.segment_sum(jnp.ones((EV_DEV,), jnp.float32), sources, num_segments=NODES_DEV)
            gate_in = summed / jnp.maximum(tallies, 1.0)[:, None]
            written = gru_update(gate_in, gate_block, start_block).astype(jnp.bfloat16)
            touched = tallies > 0.0
            current_src = current_block[sources]
            queries = jnp.dot(current_src, query_weight, preferred_element_type=jnp.float32).astype(jnp.bfloat16)
            age_values = event_times[:, None] - past_times
            keyval = (memory_keys[nbr_nodes] + time_keys[age_values]).astype(jnp.bfloat16)
            keyval = keyval.reshape(EV_DEV, NBR, 2, HEADS, head_width)
            key_heads = keyval[:, :, 0].astype(jnp.float32)
            value_heads = keyval[:, :, 1].astype(jnp.float32)
            query_heads = queries.reshape(EV_DEV, HEADS, head_width).astype(jnp.float32)
            scores = jnp.einsum('ehc,enhc->ehn', query_heads, key_heads) / jnp.sqrt(jnp.float32(head_width))
            weights = jax.nn.softmax(scores, axis=-1).astype(jnp.bfloat16)
            attended = jnp.einsum('ehn,enhc->ehc', weights.astype(jnp.float32), value_heads)
            attended = attended.reshape(EV_DEV, D_MEM).astype(jnp.bfloat16)
            embedding = jnp.dot(attended, out_weight[:D_MEM], preferred_element_type=jnp.float32)
            embedding = embedding + jnp.dot(current_src, out_weight[D_MEM:], preferred_element_type=jnp.float32)
            embedding = jax.nn.relu(embedding + bias_out).astype(jnp.bfloat16)
            embed_part = jnp.dot(embedding, pred_weight[:D_MEM], preferred_element_type=jnp.float32)

            def predict(other_mem):
                hidden_pred = embed_part + jnp.dot(other_mem, pred_weight[D_MEM:], preferred_element_type=jnp.float32)
                hidden_pred = jax.nn.relu(hidden_pred + bias_pred).astype(jnp.bfloat16)
                return jnp.dot(hidden_pred, logit_weight, preferred_element_type=jnp.float32)
            pair_logits = jnp.stack([predict(target_mem), predict(memory_start[neg_nodes])])
            return (pair_logits, written, touched)
        pair_logits, written, touched = lax.map(device_step, jnp.arange(OWNERS, dtype=jnp.int32))
        written = written.reshape(NODES, D_MEM)
        touched = touched.reshape(NODES)
        current = jnp.where(touched[:, None], written, current)
        all_memory.append(current)
        all_logits.append(jnp.transpose(pair_logits, (1, 0, 2)).reshape(2, BATCH))
    return (jnp.stack(all_logits, axis=1), jnp.stack(all_memory))
```

```python
import jax
import jax.numpy as jnp
from jax import lax
from jax.experimental import pallas as pl
from jax.experimental.pallas import tpu as pltpu
from jax.sharding import Mesh, PartitionSpec as P

HEADS = 2
TILE = 128
PLANE = ("x", "c", "y", "zp")
VMEM = pl.BlockSpec(memory_space=pltpu.VMEM)
SMEM = pl.BlockSpec(memory_space=pltpu.SMEM)
F32 = jnp.float32
BF16 = jnp.bfloat16


def params(mib):
    return pltpu.CompilerParams(vmem_limit_bytes=mib * 2**20)


def dot(a, b):
    return jnp.dot(a, b, preferred_element_type=F32)


def time_code(delta, time_freq, time_phase):
    angle = delta.astype(F32)[..., None] * time_freq + time_phase
    return jnp.cos(angle).astype(BF16)


def select_kernel(req_ref, ring_ref, left_ref, right_ref):
    dests, blocks = left_ref.shape[:2]
    half = left_ref.shape[3]

    def body(dest, carry):
        for block in range(blocks):
            tile = req_ref[dest * blocks + block]
            left_ref[dest, block] = ring_ref[block, tile, :, :half]
            right_ref[dest, block] = ring_ref[block, tile, :, half:]
        return carry

    lax.fori_loop(0, dests, body, 0)


def select_tiles(requests, ring):
    blocks, _, rows, width = ring.shape
    dests = requests.shape[0]
    out = jax.ShapeDtypeStruct((dests, blocks, rows, width // 2), ring.dtype)
    return pl.pallas_call(
        select_kernel,
        out_shape=(out, out),
        in_specs=[SMEM, VMEM],
        out_specs=(VMEM, VMEM),
        compiler_params=params(40),
        cost_estimate=pl.CostEstimate(flops=0, bytes_accessed=6 * 2**20, transcendentals=0),
    )(requests.reshape(-1), ring)


def gather_rows(index_ref, table, out, count, unroll=32):
    def body(step, carry):
        first = pl.multiple_of(step * unroll, unroll)
        for lane in range(unroll):
            row = index_ref[first + lane]
            out[pl.ds(first + lane, 1), :] = table[pl.ds(row, 1), :]
        return carry

    lax.fori_loop(0, count // unroll, body, 0)


def widen(source_ref, wide, chunk=512):
    def body(step, carry):
        at = pl.ds(pl.multiple_of(step * chunk, chunk), chunk)
        wide[at, :] = source_ref[at, :].astype(F32)
        return carry

    lax.fori_loop(0, wide.shape[0] // chunk, body, 0)


def gather_kernel(index_ref, table_ref, out_ref, wide, picked):
    count = out_ref.shape[0]
    widen(table_ref, wide)
    gather_rows(index_ref, wide, picked, count)

    def body(step, carry):
        at = pl.ds(pl.multiple_of(step * 512, 512), 512)
        out_ref[at, :] = picked[at, :].astype(BF16)
        return carry

    lax.fori_loop(0, count // 512, body, 0)


def gather_half(index, table):
    count = index.shape[0]
    rows, width = table.shape
    return pl.pallas_call(
        gather_kernel,
        out_shape=jax.ShapeDtypeStruct((count, width), BF16),
        in_specs=[SMEM, VMEM],
        out_specs=VMEM,
        scratch_shapes=[pltpu.VMEM((rows, width), F32), pltpu.VMEM((count, width), F32)],
        compiler_params=params(40),
        cost_estimate=pl.CostEstimate(flops=0, bytes_accessed=30 * 2**20, transcendentals=0),
    )(index, table)


def update_kernel(index_ref, table_ref, left_ref, base_ref, hid_ref, same_ref, source_ref, weight_ref, written_ref, right_ref, wide, picked):
    events, half = left_ref.shape[0] // 2, left_ref.shape[1]
    width = 2 * half
    widen(table_ref, wide)
    gather_rows(index_ref, wide, picked, 2 * events)
    right_ref[...] = picked[...].astype(BF16)
    target = jnp.concatenate([left_ref[:events, :], right_ref[:events, :]], axis=1)
    pre = base_ref[...] + dot(target, weight_ref[...])
    same = same_ref[...]
    tally = jnp.sum(same, axis=1, keepdims=True)
    summed = jnp.dot(same, pre, preferred_element_type=F32, precision=lax.Precision.HIGHEST)
    gate_in = summed / tally
    hid = hid_ref[...]
    reset = jax.nn.sigmoid(gate_in[:, :width] + hid[:, :width])
    keep = jax.nn.sigmoid(gate_in[:, width : 2 * width] + hid[:, width : 2 * width])
    cand = jnp.tanh(gate_in[:, 2 * width :] + reset * hid[:, 2 * width :])
    state = source_ref[...].astype(F32)
    written_ref[...] = ((1.0 - keep) * cand + keep * state).astype(BF16)


def update_rows(index, table, left, base, hid, same, source, weight):
    events, width = source.shape
    rows, half = table.shape
    return pl.pallas_call(
        update_kernel,
        out_shape=(
            jax.ShapeDtypeStruct((events, width), BF16),
            jax.ShapeDtypeStruct((2 * events, half), BF16),
        ),
        in_specs=[SMEM] + [VMEM] * 7,
        out_specs=(VMEM, VMEM),
        scratch_shapes=[pltpu.VMEM((rows, half), F32), pltpu.VMEM((2 * events, half), F32)],
        compiler_params=params(40),
        cost_estimate=pl.CostEstimate(flops=10**9, bytes_accessed=12 * 2**20, transcendentals=0),
    )(index, table, left, base, hid, same, source, weight)


def keyval_kernel(index_ref, table_ref, left_ref, code_ref, weight_ref, out_ref, wide, picked):
    count = out_ref.shape[0]
    widen(table_ref, wide)
    gather_rows(index_ref, wide, picked, count)
    weight = weight_ref[...]

    def body(step, carry):
        at = pl.ds(pl.multiple_of(step * 256, 256), 256)
        joined = jnp.concatenate(
            [left_ref[at, :], picked[at, :].astype(BF16), code_ref[at, :]], axis=1
        )
        out_ref[at, :] = dot(joined, weight).astype(BF16)
        return carry

    lax.fori_loop(0, count // 256, body, 0)


def keyval_rows(index, table, left, code, weight):
    count = index.shape[0]
    rows, half = table.shape
    return pl.pallas_call(
        keyval_kernel,
        out_shape=jax.ShapeDtypeStruct((count, weight.shape[1]), BF16),
        in_specs=[SMEM] + [VMEM] * 4,
        out_specs=VMEM,
        scratch_shapes=[pltpu.VMEM((rows, half), F32), pltpu.VMEM((count, half), F32)],
        compiler_params=params(48),
        cost_estimate=pl.CostEstimate(
            flops=2 * count * weight.shape[0] * weight.shape[1],
            bytes_accessed=40 * 2**20,
            transcendentals=0,
        ),
    )(index, table, left, code, weight)


def attend_kernel(
    latest_ref,
    rows_ref,
    source_ref,
    query_ref,
    keyval_ref,
    left_ref,
    right_ref,
    out_weight_ref,
    bias_out_ref,
    pred_ref,
    bias_pred_ref,
    logit_ref,
    logits_ref,
    queries,
    attended,
):
    events, width = source_ref.shape
    head = width // HEADS
    neighbours = keyval_ref.shape[0] // events
    latest = latest_ref[...]
    lanes = lax.broadcasted_iota(jnp.int32, (events, TILE), 1)
    hot = jnp.concatenate(
        [
            (latest == lanes + first).astype(F32).astype(BF16)
            for first in range(0, rows_ref.shape[0], TILE)
        ],
        axis=1,
    )
    moved = dot(hot, rows_ref[...])
    known = jnp.concatenate([latest] * HEADS, axis=1) >= 0
    current = jnp.where(known, moved, source_ref[...].astype(F32)).astype(BF16)
    queries[...] = dot(current, query_ref[...]).astype(BF16).astype(F32)
    group = 8
    columns = group * neighbours
    owner = lax.broadcasted_iota(jnp.int32, (HEADS * group, columns), 1) // neighbours
    event = lax.broadcasted_iota(jnp.int32, (HEADS * group, columns), 0) % group
    own = owner == event
    low = lax.broadcasted_iota(jnp.int32, (group, width), 1) < head
    scale = 1.0 / jnp.sqrt(F32(head))

    def body(step, carry):
        at = pl.ds(pl.multiple_of(step * columns, columns), columns)
        mine = pl.ds(pl.multiple_of(step * group, group), group)
        block = queries[mine, :]
        zero = jnp.zeros_like(block)
        stacked = jnp.concatenate(
            [jnp.where(low, block, zero), jnp.where(low, zero, block)], axis=0
        ).astype(BF16)
        keys = keyval_ref[at, :width]
        scores = lax.dot_general(
            stacked, keys, (((1,), (1,)), ((), ())), preferred_element_type=F32
        )
        scores = jnp.where(own, scores * scale, -jnp.inf)
        top = jnp.max(scores, axis=1, keepdims=True)
        exponent = jnp.exp(scores - top)
        weights = (exponent / jnp.sum(exponent, axis=1, keepdims=True)).astype(BF16)
        mixed = dot(weights, keyval_ref[at, width:])
        attended[mine, :] = jnp.where(low, mixed[:group, :], mixed[group:, :])
        return carry

    lax.fori_loop(0, events // group, body, 0)
    embedding = dot(attended[...].astype(BF16), out_weight_ref[:width, :])
    embedding = embedding + dot(current, out_weight_ref[width:, :]) + bias_out_ref[...]
    embedding = jnp.maximum(embedding, 0.0).astype(BF16)
    embed_part = dot(embedding, pred_ref[:width, :])
    other = jnp.concatenate([left_ref[...], right_ref[...]], axis=1)
    other_part = dot(other, pred_ref[width:, :])
    for side in range(2):
        hidden = embed_part + other_part[side * events : (side + 1) * events, :]
        hidden = jnp.maximum(hidden + bias_pred_ref[...], 0.0).astype(BF16)
        logits_ref[side : side + 1, :] = lax.dot_general(
            logit_ref[...], hidden, (((1,), (1,)), ((), ())), preferred_element_type=F32
        )


def attend(latest, rows, source, query_weight, keyval, left, right, out_weight, bias_out, pred_weight, bias_pred, logit_weight):
    events, width = source.shape
    return pl.pallas_call(
        attend_kernel,
        out_shape=jax.ShapeDtypeStruct((2, events), F32),
        in_specs=[VMEM] * 12,
        out_specs=VMEM,
        scratch_shapes=[pltpu.VMEM((events, width), F32), pltpu.VMEM((events, width), F32)],
        compiler_params=params(40),
        cost_estimate=pl.CostEstimate(flops=10**9, bytes_accessed=12 * 2**20, transcendentals=0),
    )(latest, rows, source, query_weight, keyval, left, right, out_weight, bias_out, pred_weight, bias_pred, logit_weight)


def after_kernel(latest_ref, rows_ref, start_ref, out_ref):
    block = 256
    lanes = lax.broadcasted_iota(jnp.int32, (block, TILE), 1)
    rows = rows_ref[...]

    def body(step, carry):
        at = pl.ds(pl.multiple_of(step * block, block), block)
        latest = latest_ref[at, :]
        hot = jnp.concatenate(
            [
                (latest == lanes + first).astype(F32).astype(BF16)
                for first in range(0, rows.shape[0], TILE)
            ],
            axis=1,
        )
        moved = dot(hot, rows)
        known = jnp.concatenate([latest] * (rows.shape[1] // TILE), axis=1) >= 0
        out_ref[at, :] = jnp.where(known, moved, start_ref[at, :].astype(F32)).astype(BF16)
        return carry

    lax.fori_loop(0, out_ref.shape[0] // block, body, 0)


def memory_rows(latest, rows, start):
    return pl.pallas_call(
        after_kernel,
        out_shape=jax.ShapeDtypeStruct(start.shape, BF16),
        in_specs=[VMEM] * 3,
        out_specs=VMEM,
        compiler_params=params(40),
        cost_estimate=pl.CostEstimate(
            flops=2 * start.shape[0] * rows.shape[0] * rows.shape[1],
            bytes_accessed=5 * 2**20,
            transcendentals=0,
        ),
    )(latest, rows, start)


def shards(
    memory_start,
    src_row,
    dst_pos,
    neg_pos,
    nbr_pos,
    event_time,
    nbr_time,
    edge_feat,
    tile_req,
    tile_count,
    time_freq,
    time_phase,
    msg_memory,
    msg_time,
    msg_edge,
    bias_input,
    hid_weight,
    bias_hidden,
    query_weight,
    keyval_weight,
    out_weight,
    bias_out,
    pred_weight,
    bias_pred,
    logit_weight,
):
    nx, nc, ny, nzq, nzp = (lax.axis_size(name) for name in ("x", "c", "y", "zq", "zp"))
    batches = nx * nc
    owners = ny * nzq * nzp
    node_rows, width = memory_start.shape
    half = width // 2
    events = src_row.shape[1]
    neighbours = nbr_pos.shape[2]
    tiles = node_rows // TILE
    share = TILE // batches
    batch = lax.axis_index("x") * nc + lax.axis_index("c")

    own_share = lax.dynamic_index_in_dim(
        memory_start.reshape(tiles, batches, share, width), batch, 1, False
    )
    ring = lax.all_gather(own_share, "zq")
    wanted = tile_req.reshape(ny, nzq, nzp).transpose(0, 2, 1).reshape(1, ny * nzp, nzq)
    wanted = jnp.broadcast_to(wanted, (batches, ny * nzp, nzq)).reshape(-1, nzq)
    asked = lax.all_to_all(wanted, PLANE, 0, 0, tiled=True)
    send_left, send_right = select_tiles(asked, ring)
    left_table = lax.all_to_all(send_left, PLANE, 0, 0, tiled=True).reshape(-1, half)
    right_table = lax.all_to_all(send_right, PLANE, 0, 0, tiled=True).reshape(-1, half)

    running = jnp.cumsum(tile_count.reshape(owners))

    def table_rows(position):
        owner = jnp.sum((running <= (position // TILE)[..., None]).astype(jnp.int32), axis=-1)
        row = position % TILE
        oy, ozq, ozp = owner // (nzq * nzp), (owner // nzp) % nzq, owner % nzp
        source = ((row // share) * ny + oy) * nzp + ozp
        return (source * nzq + ozq) * share + row % share

    dst_rows = table_rows(dst_pos.reshape(events))
    neg_rows = table_rows(neg_pos.reshape(events))
    nbr_rows = table_rows(nbr_pos.reshape(events * neighbours))
    pair_rows = jnp.concatenate([dst_rows, neg_rows])

    sources = src_row.reshape(events)
    event_times = event_time.reshape(events)
    past_times = nbr_time.reshape(events, neighbours)
    ages = event_times[:, None] - past_times
    code = time_code(ages.reshape(-1), time_freq, time_phase)
    source_mem = memory_start[sources]
    base = dot(source_mem, msg_memory[:width])
    base = base + dot(time_code(ages[:, 0], time_freq, time_phase), msg_time)
    base = base + dot(edge_feat.reshape(events, -1), msg_edge)
    base = base + bias_input
    hid = dot(source_mem, hid_weight) + bias_hidden
    same = (sources[:, None] == sources[None, :]).astype(F32)
    all_sources = lax.all_gather(sources, ("x", "c")).reshape(-1)
    order = jnp.arange(batches * events, dtype=jnp.int32)
    of_batch = order // events
    node_ids = jnp.arange(node_rows, dtype=jnp.int32)
    upto = jnp.where(of_batch <= batch, all_sources, -1)
    earlier = jnp.where(of_batch < batch, all_sources, -1)
    after_row = jnp.max(jnp.where(upto[None, :] == node_ids[:, None], order[None, :], -1), axis=1)
    before_row = jnp.max(jnp.where(earlier[None, :] == sources[:, None], order[None, :], -1), axis=1)
    after_row = jnp.broadcast_to(after_row[:, None], (node_rows, TILE))
    before_row = jnp.broadcast_to(before_row[:, None], (events, TILE))

    left_rows = gather_half(jnp.concatenate([nbr_rows, pair_rows]), left_table)
    nbr_left = left_rows[: events * neighbours]
    pair_left = left_rows[events * neighbours :]
    written, pair_right = update_rows(
        pair_rows, right_table, pair_left, base, hid, same, source_mem, msg_memory[width:]
    )
    rows = lax.all_to_all(
        jnp.broadcast_to(written[None], (batches, events, width)), ("x", "c"), 0, 0, tiled=True
    ).reshape(-1, width)
    keyval = keyval_rows(nbr_rows, right_table, nbr_left, code, keyval_weight)
    logits = attend(
        before_row,
        rows,
        source_mem,
        query_weight,
        keyval,
        pair_left,
        pair_right,
        out_weight,
        bias_out.reshape(1, -1),
        pred_weight,
        bias_pred.reshape(1, -1),
        logit_weight.reshape(1, -1),
    )
    memory_after = memory_rows(after_row, rows, memory_start)
    return (logits.reshape(2, 1, events), memory_after.reshape(1, node_rows, width))


def solution(mesh):
    grid = Mesh(mesh.devices.reshape(4, 2, 4, 8, 2), ("x", "c", "y", "zq", "zp"))
    tm, dom = ("x", "c"), ("y", "zq", "zp")
    by_event = [P(tm, dom), P(tm, dom, None)]
    in_specs = (
        P(dom, None),
        by_event[0],
        by_event[0],
        by_event[0],
        by_event[1],
        by_event[0],
        by_event[1],
        by_event[1],
        by_event[1],
        by_event[1],
    ) + (P(),) * 15
    out_specs = (P(None, tm, dom), P(tm, dom, None))
    return jax.shard_map(
        shards, mesh=grid, in_specs=in_specs, out_specs=out_specs, check_vma=False
    )
```

```python
import jax
import jax.numpy as jnp
from jax import lax
from jax.experimental import pallas as pl
from jax.experimental.pallas import tpu as pltpu
from jax.sharding import Mesh, PartitionSpec as P

HEADS = 2
TILE = 128
PLANE = ("x", "c", "y", "zp")
VMEM = pl.BlockSpec(memory_space=pltpu.VMEM)
SMEM = pl.BlockSpec(memory_space=pltpu.SMEM)
ANY = pl.BlockSpec(memory_space=pl.ANY)
F32 = jnp.float32
BF16 = jnp.bfloat16


def params(mib):
    return pltpu.CompilerParams(vmem_limit_bytes=mib * 2**20)


def dot(a, b):
    return jnp.dot(a, b, preferred_element_type=F32)


def time_code(delta, time_freq, time_phase):
    angle = delta.astype(F32)[..., None] * time_freq + time_phase
    return jnp.cos(angle).astype(BF16)


def copies_of(pairs, sems):
    return [
        pltpu.make_async_copy(source, target, sems.at[place])
        for place, (source, target) in enumerate(pairs)
    ]


def start_copies(pairs, sems):
    copies = copies_of(pairs, sems)
    for copy in copies:
        copy.start()
    return copies


def select_kernel(req_ref, ring_any, out_ref, ring, sems):
    dests, blocks = out_ref.shape[:2]
    copies = start_copies(
        [(ring_any.at[block], ring.at[block]) for block in range(blocks)], sems
    )
    group = 8
    for block in range(blocks):
        copies[block].wait()

        def body(step, carry):
            for place in range(group):
                dest = step * group + place
                out_ref[dest, block] = ring[block, req_ref[dest * blocks + block]]
            return carry

        lax.fori_loop(0, dests // group, body, 0)


def select_tiles(requests, ring):
    blocks, _, rows, width = ring.shape
    dests = requests.shape[0]
    return pl.pallas_call(
        select_kernel,
        out_shape=jax.ShapeDtypeStruct((dests, blocks, rows, width), ring.dtype),
        in_specs=[SMEM, ANY],
        out_specs=VMEM,
        scratch_shapes=[pltpu.VMEM(ring.shape, ring.dtype), pltpu.SemaphoreType.DMA((blocks,))],
        compiler_params=params(16),
        cost_estimate=pl.CostEstimate(flops=0, bytes_accessed=6 * 2**20, transcendentals=0),
    )(requests.reshape(-1), ring)


def table_copies(table_any, table, sems, chunk):
    pairs = []
    for first in range(0, table.shape[0], chunk):
        at = pl.ds(first, chunk)
        pairs.append((table_any.at[at, :], table.at[at, :]))
    return start_copies(pairs, sems)


def widen(copies, table, lows, highs, chunk):
    half = lows.shape[1]
    step_rows = 128
    for place, copy in enumerate(copies):
        copy.wait()

        def body(step, carry):
            first = pl.multiple_of(place * chunk + step * step_rows, step_rows)
            at = pl.ds(first, step_rows)
            lows[at, :] = table[at, :half].astype(F32)
            highs[at, :] = table[at, half:].astype(F32)
            return carry

        lax.fori_loop(0, chunk // step_rows, body, 0)


def gather_block(index_ref, first, lows, highs, low_out, high_out):
    for lane in range(low_out.shape[0]):
        row = index_ref[first + lane]
        low_out[pl.ds(lane, 1), :] = lows[pl.ds(row, 1), :]
        high_out[pl.ds(lane, 1), :] = highs[pl.ds(row, 1), :]


CHUNKS = 8


def update_kernel(
    index_ref,
    table_any,
    base_any,
    hid_any,
    same_any,
    source_any,
    weight_any,
    written_ref,
    pair_ref,
    table,
    lows,
    highs,
    low_pick,
    high_pick,
    base,
    hid,
    same,
    source,
    weight,
    sems,
    table_sems,
):
    pairs, width = pair_ref.shape
    events = pairs // 2
    chunk = table.shape[0] // CHUNKS
    arrivals = table_copies(table_any, table, table_sems, chunk)
    copies = start_copies(
        [
            (base_any, base),
            (hid_any, hid),
            (same_any, same),
            (source_any, source),
            (weight_any, weight),
        ],
        sems,
    )
    widen(arrivals, table, lows, highs, chunk)
    block = low_pick.shape[0]

    def body(step, carry):
        first = pl.multiple_of(step * block, block)
        gather_block(index_ref, first, lows, highs, low_pick, high_pick)
        picked = jnp.concatenate([low_pick[...], high_pick[...]], axis=1)
        pair_ref[pl.ds(first, block), :] = picked.astype(BF16)
        return carry

    lax.fori_loop(0, pairs // block, body, 0)
    for copy in copies:
        copy.wait()
    pre = base[...] + dot(pair_ref[:events, :], weight[...])
    tally = jnp.sum(same[...], axis=1, keepdims=True)
    summed = jnp.dot(
        same[...], pre, preferred_element_type=F32, precision=lax.Precision.HIGHEST
    )
    gate_in = summed / tally
    reset = jax.nn.sigmoid(gate_in[:, :width] + hid[:, :width])
    keep = jax.nn.sigmoid(gate_in[:, width : 2 * width] + hid[:, width : 2 * width])
    cand = jnp.tanh(gate_in[:, 2 * width :] + reset * hid[:, 2 * width :])
    state = source[...].astype(F32)
    written_ref[...] = ((1.0 - keep) * cand + keep * state).astype(BF16)


def update_rows(index, table, base, hid, same, source, weight):
    events, width = source.shape
    rows = table.shape[0]
    half, block = width // 2, 64
    held = [base, hid, same, source, weight]
    return pl.pallas_call(
        update_kernel,
        out_shape=(
            jax.ShapeDtypeStruct((events, width), BF16),
            jax.ShapeDtypeStruct((2 * events, width), BF16),
        ),
        in_specs=[SMEM] + [ANY] * 6,
        out_specs=(VMEM, VMEM),
        scratch_shapes=[
            pltpu.VMEM((rows, width), BF16),
            pltpu.VMEM((rows, half), F32),
            pltpu.VMEM((rows, half), F32),
            pltpu.VMEM((block, half), F32),
            pltpu.VMEM((block, half), F32),
        ]
        + [pltpu.VMEM(array.shape, array.dtype) for array in held]
        + [pltpu.SemaphoreType.DMA((len(held),)), pltpu.SemaphoreType.DMA((CHUNKS,))],
        compiler_params=params(24),
        cost_estimate=pl.CostEstimate(flops=10**9, bytes_accessed=8 * 2**20, transcendentals=0),
    )(index, table, *held)


def keyval_kernel(
    index_ref,
    table_any,
    code_any,
    weight_any,
    out_any,
    table,
    lows,
    highs,
    even_low,
    even_high,
    odd_low,
    odd_high,
    code,
    weight,
    out,
    sems,
    table_sems,
    out_sems,
):
    count = out.shape[0]
    block = even_low.shape[0]
    pairs = count // (2 * block)
    chunk = table.shape[0] // CHUNKS
    arrivals = table_copies(table_any, table, table_sems, chunk)
    copies = start_copies([(code_any, code), (weight_any, weight)], sems)
    widen(arrivals, table, lows, highs, chunk)

    def project(first, low, high):
        at = pl.ds(first, block)
        joined = [low[...].astype(BF16), high[...].astype(BF16), code[at, :]]
        out[at, :] = dot(jnp.concatenate(joined, axis=1), weight[...]).astype(BF16)

    def saved(step):
        at = pl.ds(pl.multiple_of(step * 2 * block, 2 * block), 2 * block)
        return pltpu.make_async_copy(out.at[at, :], out_any.at[at, :], out_sems.at[step])

    gather_block(index_ref, 0, lows, highs, even_low, even_high)
    for copy in copies:
        copy.wait()

    def body(step, carry):
        first = pl.multiple_of(step * 2 * block, 2 * block)
        second = pl.multiple_of(first + block, block)
        gather_block(index_ref, second, lows, highs, odd_low, odd_high)
        project(first, even_low, even_high)
        third = pl.multiple_of(jnp.where(step + 1 < pairs, first + 2 * block, 0), block)
        gather_block(index_ref, third, lows, highs, even_low, even_high)
        project(second, odd_low, odd_high)
        saved(step).start()
        return carry

    lax.fori_loop(0, pairs, body, 0)

    def finish(step, carry):
        saved(step).wait()
        return carry

    lax.fori_loop(0, pairs, finish, 0)


def keyval_rows(index, table, code, weight):
    count = index.shape[0]
    rows, width = table.shape
    half, block = width // 2, 512
    out = jax.ShapeDtypeStruct((count, weight.shape[1]), BF16)
    return pl.pallas_call(
        keyval_kernel,
        out_shape=out,
        in_specs=[SMEM] + [ANY] * 3,
        out_specs=ANY,
        scratch_shapes=[
            pltpu.VMEM((rows, width), BF16),
            pltpu.VMEM((rows, half), F32),
            pltpu.VMEM((rows, half), F32),
            pltpu.VMEM((block, half), F32),
            pltpu.VMEM((block, half), F32),
            pltpu.VMEM((block, half), F32),
            pltpu.VMEM((block, half), F32),
            pltpu.VMEM(code.shape, BF16),
            pltpu.VMEM(weight.shape, BF16),
            pltpu.VMEM(out.shape, BF16),
            pltpu.SemaphoreType.DMA((2,)),
            pltpu.SemaphoreType.DMA((CHUNKS,)),
            pltpu.SemaphoreType.DMA((count // (2 * block),)),
        ],
        compiler_params=params(32),
        cost_estimate=pl.CostEstimate(
            flops=2 * count * weight.shape[0] * weight.shape[1],
            bytes_accessed=16 * 2**20,
            transcendentals=0,
        ),
    )(index, table, code, weight)


def one_hot(row, total):
    behind = row - lax.broadcasted_iota(jnp.int32, row.shape, 1)
    return jnp.concatenate(
        [jnp.where(behind == first, 1.0, 0.0).astype(BF16) for first in range(0, total, TILE)],
        axis=1,
    )


def newest(row, rows, held):
    known = jnp.concatenate([row] * (rows.shape[1] // TILE), axis=1) >= 0
    return jnp.where(known, dot(one_hot(row, rows.shape[0]), rows), held.astype(F32)).astype(BF16)


def final_kernel(
    rows_any,
    before_any,
    source_any,
    weight_any,
    after_any,
    start_any,
    keyval_any,
    pair_any,
    small_any,
    logits_ref,
    memory_any,
    rows,
    before,
    source,
    weight,
    after,
    start,
    keyval_ref,
    pair,
    small,
    memory,
    queries,
    attended,
    sems,
):
    events, width = source.shape
    head = width // HEADS
    neighbours = keyval_ref.shape[0] // events
    copies = start_copies(
        [
            (before_any, before),
            (rows_any, rows),
            (source_any, source),
            (weight_any, weight),
            (after_any, after),
            (start_any, start),
            (keyval_any, keyval_ref),
            (pair_any, pair),
            (small_any, small),
        ],
        sems,
    )
    for copy in copies[:3]:
        copy.wait()
    current = newest(before[...], rows[...], source[...])
    copies[3].wait()
    queries[...] = dot(current, weight[:width, :]).astype(BF16).astype(F32)
    copies[4].wait()
    copies[5].wait()
    block = 1024

    def update(step, carry):
        at = pl.ds(pl.multiple_of(step * block, block), block)
        memory[at, :] = newest(after[at, :], rows[...], start[at, :])
        return carry

    lax.fori_loop(0, memory.shape[0] // block, update, 0)
    saved = pltpu.make_async_copy(memory, memory_any, sems.at[9])
    saved.start()
    for copy in copies[6:]:
        copy.wait()

    group, batch = 8, 8
    columns = group * neighbours
    owner = lax.broadcasted_iota(jnp.int32, (HEADS * group, columns), 1) // neighbours
    event = lax.broadcasted_iota(jnp.int32, (HEADS * group, columns), 0) % group
    own = owner == event
    low = lax.broadcasted_iota(jnp.int32, (group, width), 1) < head
    scale = 1.0 / jnp.sqrt(F32(head))

    def body(step, carry):
        firsts = [step * batch + place for place in range(batch)]
        ats = [pl.ds(pl.multiple_of(first * columns, columns), columns) for first in firsts]
        lines = [pl.ds(pl.multiple_of(first * group, group), group) for first in firsts]
        scores = []
        for at, line in zip(ats, lines):
            query = queries[line, :]
            zero = jnp.zeros_like(query)
            stacked = jnp.concatenate(
                [jnp.where(low, query, zero), jnp.where(low, zero, query)], axis=0
            ).astype(BF16)
            scores.append(
                lax.dot_general(
                    stacked,
                    keyval_ref[at, :width],
                    (((1,), (1,)), ((), ())),
                    preferred_element_type=F32,
                )
            )
        scores = [jnp.where(own, score * scale, -jnp.inf) for score in scores]
        tops = [jnp.max(score, axis=1, keepdims=True) for score in scores]
        powers = [jnp.exp(score - top) for score, top in zip(scores, tops)]
        totals = [jnp.sum(power, axis=1, keepdims=True) for power in powers]
        shares = [(power / total).astype(BF16) for power, total in zip(powers, totals)]
        mixes = [dot(part, keyval_ref[at, width:]) for part, at in zip(shares, ats)]
        for mixed, line in zip(mixes, lines):
            attended[line, :] = jnp.where(low, mixed[:group, :], mixed[group:, :])
        return carry

    lax.fori_loop(0, events // group // batch, body, 0)
    embedding = dot(attended[...].astype(BF16), weight[width : 2 * width, :])
    embedding = embedding + dot(current, weight[2 * width : 3 * width, :]) + small[0:1, :]
    embedding = jnp.maximum(embedding, 0.0).astype(BF16)
    embed_part = dot(embedding, weight[3 * width : 4 * width, :])
    other_part = dot(pair[...], weight[4 * width :, :])
    for side in range(2):
        hidden = embed_part + other_part[side * events : (side + 1) * events, :]
        hidden = jnp.maximum(hidden + small[1:2, :], 0.0).astype(BF16)
        logits_ref[side : side + 1, :] = lax.dot_general(
            small[2:3, :].astype(BF16),
            hidden,
            (((1,), (1,)), ((), ())),
            preferred_element_type=F32,
        )
    saved.wait()


def final_step(*held):
    rows, before, source, weight, after, start, keyval, pair, small = held
    events, width = source.shape
    return pl.pallas_call(
        final_kernel,
        out_shape=(
            jax.ShapeDtypeStruct((2, events), F32),
            jax.ShapeDtypeStruct(start.shape, BF16),
        ),
        in_specs=[ANY] * len(held),
        out_specs=(VMEM, ANY),
        scratch_shapes=[pltpu.VMEM(array.shape, array.dtype) for array in held]
        + [
            pltpu.VMEM(start.shape, BF16),
            pltpu.VMEM((events, width), F32),
            pltpu.VMEM((events, width), F32),
            pltpu.SemaphoreType.DMA((len(held) + 1,)),
        ],
        compiler_params=params(28),
        cost_estimate=pl.CostEstimate(
            flops=4 * 10**9, bytes_accessed=12 * 2**20, transcendentals=0
        ),
    )(*held)


def shards(
    memory_start,
    src_row,
    dst_pos,
    neg_pos,
    nbr_pos,
    event_time,
    nbr_time,
    edge_feat,
    tile_req,
    tile_count,
    time_freq,
    time_phase,
    msg_memory,
    msg_time,
    msg_edge,
    bias_input,
    hid_weight,
    bias_hidden,
    query_weight,
    keyval_weight,
    out_weight,
    bias_out,
    pred_weight,
    bias_pred,
    logit_weight,
):
    nx, nc, ny, nzq, nzp = (lax.axis_size(name) for name in ("x", "c", "y", "zq", "zp"))
    batches = nx * nc
    owners = ny * nzq * nzp
    node_rows, width = memory_start.shape
    events = src_row.shape[1]
    neighbours = nbr_pos.shape[2]
    tiles = node_rows // TILE
    share = TILE // batches
    batch = lax.axis_index("x") * nc + lax.axis_index("c")

    own_share = lax.dynamic_index_in_dim(
        memory_start.reshape(tiles, batches, share, width), batch, 1, False
    )
    sources = src_row.reshape(events)
    wanted = tile_req.reshape(ny, nzq, nzp).transpose(0, 2, 1).reshape(1, ny * nzp, nzq)
    wanted = jnp.broadcast_to(wanted, (batches, ny * nzp, nzq)).reshape(-1, nzq)
    told = jnp.broadcast_to(sources[None], (wanted.shape[0], events))
    heard = lax.all_to_all(
        jnp.concatenate([wanted, told], axis=1), PLANE, 0, 0, tiled=True
    )
    asked = heard[:, :nzq]
    heard = heard[:, nzq:].reshape(batches, ny, nzp, events)
    heard = lax.dynamic_index_in_dim(heard, lax.axis_index("y"), 1, False)
    all_sources = lax.dynamic_index_in_dim(heard, lax.axis_index("zp"), 1, False).reshape(-1)

    running = jnp.cumsum(tile_count.reshape(owners))

    def table_rows(position):
        owner = jnp.sum((running <= (position // TILE)[..., None]).astype(jnp.int32), axis=-1)
        row = position % TILE
        oy, ozq, ozp = owner // (nzq * nzp), (owner // nzp) % nzq, owner % nzp
        source = ((row // share) * ny + oy) * nzp + ozp
        return (source * nzq + ozq) * share + row % share

    dst_rows = table_rows(dst_pos.reshape(events))
    neg_rows = table_rows(neg_pos.reshape(events))
    nbr_rows = table_rows(nbr_pos.reshape(events * neighbours))
    pair_rows = jnp.concatenate([dst_rows, neg_rows])

    event_times = event_time.reshape(events)
    past_times = nbr_time.reshape(events, neighbours)
    ages = event_times[:, None] - past_times
    code = time_code(ages.reshape(-1), time_freq, time_phase)
    source_mem = memory_start[sources]
    base = dot(source_mem, msg_memory[:width])
    base = base + dot(time_code(ages[:, 0], time_freq, time_phase), msg_time)
    base = base + dot(edge_feat.reshape(events, -1), msg_edge)
    base = base + bias_input
    hid = dot(source_mem, hid_weight) + bias_hidden
    same = (sources[:, None] == sources[None, :]).astype(F32)
    order = jnp.arange(batches * events, dtype=jnp.int32)
    of_batch = order // events
    node_ids = jnp.arange(node_rows, dtype=jnp.int32)
    upto = jnp.where(of_batch <= batch, all_sources, -1)
    earlier = jnp.where(of_batch < batch, all_sources, -1)
    after_row = jnp.max(jnp.where(upto[None, :] == node_ids[:, None], order[None, :], -1), axis=1)
    before_row = jnp.max(jnp.where(earlier[None, :] == sources[:, None], order[None, :], -1), axis=1)
    after_row = jnp.broadcast_to(after_row[:, None], (node_rows, TILE))
    before_row = jnp.broadcast_to(before_row[:, None], (events, TILE))

    weights = jnp.concatenate([query_weight, out_weight, pred_weight])
    small = jnp.stack([bias_out, bias_pred, logit_weight.astype(F32)])
    small = jnp.concatenate([small, jnp.zeros((5, width), F32)])
    target_weight = msg_memory[width:]

    ring = lax.all_gather(own_share, "zq")
    table = lax.all_to_all(select_tiles(asked, ring), PLANE, 0, 0, tiled=True)
    table = table.reshape(-1, width)
    base, after_row, before_row = lax.optimization_barrier((base, after_row, before_row))
    written, pair = update_rows(pair_rows, table, base, hid, same, source_mem, target_weight)
    rows = lax.all_to_all(
        jnp.broadcast_to(written[None], (batches, events, width)), ("x", "c"), 0, 0, tiled=True
    ).reshape(-1, width)
    keyval = keyval_rows(nbr_rows, table, code, keyval_weight)
    logits, memory_after = final_step(
        rows,
        before_row,
        source_mem,
        weights,
        after_row,
        memory_start,
        keyval,
        pair,
        small,
    )
    return (logits.reshape(2, 1, events), memory_after.reshape(1, node_rows, width))


def solution(mesh):
    grid = Mesh(mesh.devices.reshape(4, 2, 4, 8, 2), ("x", "c", "y", "zq", "zp"))
    tm, dom = ("x", "c"), ("y", "zq", "zp")
    by_event = [P(tm, dom), P(tm, dom, None)]
    in_specs = (
        P(dom, None),
        by_event[0],
        by_event[0],
        by_event[0],
        by_event[1],
        by_event[0],
        by_event[1],
        by_event[1],
        by_event[1],
        by_event[1],
    ) + (P(),) * 15
    out_specs = (P(None, tm, dom), P(tm, dom, None))
    return jax.shard_map(
        shards, mesh=grid, in_specs=in_specs, out_specs=out_specs, check_vma=False
    )
```
